256 devices in a mesh: sector: 32 (over x, z), term: 8 (over y, core).
Axes of the slice: x: 4, y: 4, z: 8, core: 2. Of those that a mesh axis runs over, the one named last changes fastest.
Arguments:
- wavefunction: bfloat16 [256, 256, 256], P('sector', 'term'), may hold values from -6 to 6
- left_ops: bfloat16 [64, 256, 256, 256], P('term', 'sector'), may hold values from -0.375 to 0.375
- right_ops: bfloat16 [64, 256, 256], P('term'), may hold values from -0.046875 to 0.046875
- term_type: int32 [64], P('term'), may hold values from 0 to 1
- target_slots: int32 [2, 256], replicated, may hold values from 0 to 255, as said below
- block_rows: int32 [256], replicated, may hold values from 1 to 256, 32768 in all
Outputs:
- sigma_blocks: bfloat16 [256, 256, 256], P('sector', 'term')
The draws below stay inside these ranges and needn't reach their ends.
Inputs may be any that keep to these rules, and one draw needn't show every extreme that they name: Each row target_slots[g] is a permutation of the 256 slots. Slots i * 8 to (i + 1) * 8 - 1 lie on device i of the sector axis, and the 16 entries of one device's slots (both rows together) name slots of any one device at most 1 times; that most is reached. `block_rows`: some block uses all 256 rows.
All inputs are finite; a program needn't handle non-finite values.
Results may differ from the reference program's by a relative error of at most 0.0049.
Values may be sent and summed in bfloat16 or wider, within the bound.
A program may use at most 128 MiB of HBM per device.

```python
import math
import jax
import jax.numpy as jnp
import numpy as np
from jax import lax

BL = 256
BR = 256
TYPES = 2
SEC_DEV = 8
NSEC = 256
TERMS = 64


def draw_target_slots(key, part):
    key = jax.random.fold_in(key, 7)
    group_count = NSEC // SEC_DEV
    item_count = TYPES * SEC_DEV
    per_peer = max(1, item_count // group_count)
    key_relabel, key_start, key_offset, key_local = jax.random.split(key, 4)
    relabel = jax.random.permutation(key_relabel, group_count)
    starting = jax.random.permutation(key_start, group_count)
    offsets = jax.random.permutation(key_offset, group_count)
    item_ids = jnp.arange(item_count)
    target_dev = relabel[(starting[:, None] + offsets[item_ids // per_peer][None, :]) % group_count]
    local_keys = jax.random.split(key_local, TYPES)
    local_slots = jnp.stack([jax.random.permutation(local_keys[index], SEC_DEV) for index in range(TYPES)])
    slots = target_dev * SEC_DEV + local_slots.reshape(-1)[None, :]
    slots = slots.reshape(group_count, TYPES, SEC_DEV).transpose(1, 0, 2).reshape(TYPES, NSEC)
    return slots.astype(jnp.int32)


def plant(result, rng, least, largest):
    longest = result.shape.index(max(result.shape))
    spots = []
    for shift in (0, 1):
        where = [jax.random.randint(jax.random.fold_in(rng, axis), (), 0, length) for axis, length in enumerate(result.shape)]
        where[longest] = (where[longest] + shift) % result.shape[longest]
        spots.append(tuple(where))
    return result.at[spots[0]].set(least).at[spots[1]].set(largest)


def block_levels(stream_key, shape, pieces, least, largest):
    def one(axis_at, shards_of):
        steps = jax.random.uniform(jax.random.fold_in(jax.random.fold_in(stream_key, 6), axis_at), (shards_of,), jnp.float32, least / len(pieces), largest / len(pieces))
        return jnp.repeat(jnp.exp(steps), shape[axis_at] // shards_of).reshape((-1,) + (1,) * (len(shape) - axis_at - 1))

    gain = one(*pieces[0])
    for cut in pieces[1:]:
        gain = gain * one(*cut)
    return gain


def length_profile(amount, total, most, slope):
    weights = [(1 << 20) // math.isqrt(grade ** slope) + 1 for grade in range(2, amount + 1)]
    rest, given = total - most - (amount - 1), [1] * (amount - 1)
    while rest > 0:
        free = [i for i in range(amount - 1) if given[i] < most]
        whole, budget = sum([weights[i] for i in free]), rest
        for i in free:
            extra = min(most - given[i], max(1, budget * weights[i] // whole), rest)
            given[i] = given[i] + extra
            rest = rest - extra
    return np.array([most] + given)


def uneven(own_key, number_of, total, bound, slope):
    if number_of == 2:
        one = jax.random.randint(own_key, (), max(1, total - bound), min(bound, total - 1) + 1)
        return jnp.stack([one, total - one])
    sizes = jnp.asarray(length_profile(number_of, total, bound, slope), jnp.int32)
    couples = (number_of - 1) // 2
    giver, sink = sizes[1:1 + 2 * couples:2], sizes[2:2 + 2 * couples:2]
    room = jnp.minimum(giver - 1, bound - sink)
    shifted = jax.random.randint(jax.random.fold_in(own_key, 1), (couples,), 0, 1 << 20) % (room + 1)
    sizes = sizes.at[1:1 + 2 * couples:2].set(giver - shifted).at[2:2 + 2 * couples:2].set(sink + shifted)
    return sizes[jax.random.permutation(jax.random.fold_in(own_key, 2), number_of)]


def centred(own_key, dims, scale, most, pieces=(), kind=jnp.bfloat16):
    gain = block_levels(own_key, dims, pieces, -0.22, 0.18) if pieces else 1.0
    entries = jax.random.normal(own_key, dims, jnp.float32) * scale * gain
    return jnp.minimum(jnp.maximum(entries, -most), most).astype(kind)


def setup_inputs(seed: int = 0) -> dict:
    key_list = jax.random.split(jax.random.key(seed), 7)
    return {
        "wavefunction": centred(key_list[0], (NSEC, BL, BR), 1.0, 6.0, ((0, 32), (1, 8))),
        "left_ops": centred(key_list[1], (TERMS, NSEC, BL, BL), BL ** -0.5, 0.375, ((0, 8), (1, 32))),
        "right_ops": centred(key_list[2], (TERMS, BR, BR), (BR * TERMS) ** -0.5, 0.046875, ((0, 8),)),
        "term_type": plant(jax.random.randint(key_list[3], (TERMS,), 0, 2), jax.random.fold_in(key_list[3], 1), 0, 1).astype(jnp.int32),
        "target_slots": draw_target_slots(jax.random.fold_in(key_list[6], 71), 0),
        "block_rows": uneven(key_list[5], NSEC, NSEC * BL // 2, BL, 2).astype(jnp.int32),
    }


def reference(wavefunction, left_ops, right_ops, term_type, target_slots, block_rows):
    row_ids = jnp.arange(BL, dtype=jnp.int32)
    row_mask = row_ids[None, :] < block_rows[:, None]
    masked = jnp.where(row_mask[:, :, None], wavefunction, jnp.zeros((), wavefunction.dtype))

    def add_term(totals, inputs):
        left_block, right_block, op_type = inputs
        half_step = jnp.einsum("sab,sbc->sac", left_block.astype(jnp.float32), masked.astype(jnp.float32)).astype(jnp.bfloat16)
        term_block = jnp.einsum("sac,cd->sad", half_step.astype(jnp.float32), right_block.astype(jnp.float32))
        updated = lax.dynamic_index_in_dim(totals, op_type, 0, keepdims=False) + term_block
        return lax.dynamic_update_index_in_dim(totals, updated, op_type, 0), None

    initial = jnp.zeros((TYPES, NSEC, BL, BR), jnp.float32)
    contrib, _ = lax.scan(add_term, initial, (left_ops, right_ops, term_type))
    sigma_sum = jnp.zeros((NSEC, BL, BR), jnp.float32)
    for op_type in range(TYPES):
        sigma_sum = sigma_sum.at[target_slots[op_type]].add(contrib[op_type])
    sigma_sum = jnp.where(row_mask[:, :, None], sigma_sum, jnp.zeros((), sigma_sum.dtype))
    return sigma_sum.astype(jnp.bfloat16)
```

```python
import jax
import jax.numpy as jnp
from jax import lax
from jax.experimental import pallas as pl
from jax.experimental.pallas import tpu as pltpu
from jax.sharding import PartitionSpec as P

MESH = pl.DeviceIdType.MESH
BF, F32 = jnp.bfloat16, jnp.float32
N = 256
S = 8
K = 8
G = 2
Y = 4
J = 8
D = 32
H = 2
R = N // J // H
C = 2
SC = S // C


def kernel(
    wf, left, right, types, slots, rows,
    out,
    left_v, right_v, rcat, gath, masked, half, own, d2d_out, d2d_in, y_out, y_in,
    items, a2a_out, a2a_in, tab_v, tab,
    left_sem, misc_sem, ag_send, ag_recv, d2d_send, d2d_recv, y_send, y_recv, a2a_send, a2a_recv,
):
    me_s, me_t = lax.axis_index("sector"), lax.axis_index("term")
    y, c = me_t // 2, me_t % 2
    sib = y * 2 + (1 - c)

    def term_copy(src, dst, send, recv, to):
        return pltpu.make_async_remote_copy(
            src_ref=src, dst_ref=dst, send_sem=send, recv_sem=recv,
            device_id={"term": to}, device_id_type=MESH,
        )

    def y_peer(d):
        return lax.rem(y + d, Y) * 2 + c

    right_copy = pltpu.make_async_copy(right, right_v, misc_sem.at[0])
    right_copy.start()
    left_copies = {}
    for h in range(H):
        for o in range(2):
            side = 1 - c if o == 0 else c
            for s in range(S):
                cp = pltpu.make_async_copy(
                    left.at[:, s, :, side, h], left_v.at[h, o, s], left_sem.at[h, o, s]
                )
                cp.start()
                left_copies[h, o, s] = cp
    own_copy = pltpu.make_async_copy(wf, gath.at[:, me_t], misc_sem.at[1])
    own_copy.start()

    barrier = pltpu.get_barrier_semaphore()
    pl.semaphore_signal(barrier, inc=1, device_id={"term": sib}, device_id_type=MESH)
    for d in range(1, Y):
        pl.semaphore_signal(barrier, inc=1, device_id={"term": y_peer(d)}, device_id_type=MESH)

    @pl.loop(1, D)
    def _(q):
        pl.semaphore_signal(
            barrier, inc=1, device_id={"sector": lax.rem(me_s + q, D)}, device_id_type=MESH
        )

    pl.semaphore_wait(barrier, 1 + (Y - 1) + (D - 1))

    pending = []
    first = {}
    for p in range(C):
        part = pl.ds(p * SC, SC)
        for d in (1, 3, 2):
            cp = term_copy(
                wf.at[part], gath.at[part, me_t], ag_send.at[p, d], ag_recv.at[p, d], y_peer(d)
            )
            cp.start()
            first[p, d] = cp
        cp = term_copy(wf.at[part], gath.at[part, me_t], ag_send.at[p, 0], ag_recv.at[p, 0], sib)
        cp.start()
        first[p, 0] = cp

    lane = lax.broadcasted_iota(jnp.int32, (D, D * S), 1)
    peer = lax.broadcasted_iota(jnp.int32, (D, D * S), 0)
    mine = lax.shift_right_logical(lane, 3) == me_s
    item = jnp.zeros((D, D * S), jnp.int32)
    target = lax.broadcasted_iota(jnp.int32, (S, D * S), 0) + me_s * S
    lane_s = lax.broadcasted_iota(jnp.int32, (S, D * S), 1)
    for g in range(G):
        row = slots[g : g + 1, :]
        hit = mine & (lax.shift_right_logical(row, 3) == peer)
        item = jnp.maximum(item, jnp.where(hit, jnp.bitwise_and(lane, 7) + g * S, 0))
        src = jnp.where(row == target, lax.shift_right_logical(lane_s, 3), 0)
        tab_v[D + g * S : D + (g + 1) * S, :] = jnp.broadcast_to(
            jnp.max(src, axis=1, keepdims=True), (S, 128)
        )
    tab_v[0:D, :] = jnp.broadcast_to(jnp.max(item, axis=1, keepdims=True), (D, 128))
    tab_copy = pltpu.make_async_copy(tab_v, tab, misc_sem.at[2])
    tab_copy.start()

    right_copy.wait()
    for k in range(K):
        for g in range(G):
            rcat[k * N : (k + 1) * N, g * N : (g + 1) * N] = jnp.where(
                types[k] == g, right_v[k].astype(F32), 0.0
            ).astype(BF)

    own_copy.wait()
    for p in range(C):
        part = pl.ds(p * SC, SC)
        for d in (1, 3, 2):
            first[p, d].wait_recv()
            owner = lax.rem(y + Y - d, Y) * 2 + c
            block = gath.at[part, owner]
            cp = term_copy(block, block, ag_send.at[p, 3 + d], ag_recv.at[p, 3 + d], sib)
            cp.start()
            first[p, 3 + d] = cp
        first[p, 0].wait_recv()
        for d in (1, 3, 2):
            first[p, 3 + d].wait_recv()
        for s in range(p * SC, (p + 1) * SC):
            row_id = lax.broadcasted_iota(jnp.int32, (N, N), 0)
            block = gath[s].reshape(N, N).astype(F32)
            masked[s] = jnp.where(row_id < rows[me_s * S + s], block, 0.0).astype(BF)
    pending += list(first.values())

    def unit(h, o):
        for s in range(S):
            left_copies[h, o, s].wait()

        @pl.loop(0, S)
        def _(s):
            lhs = left_v[h, o, s].reshape(K * Y * R, N)
            res = jnp.dot(lhs, masked[s], preferred_element_type=F32).astype(BF)
            for k in range(K):
                half[s, :, k * N : (k + 1) * N] = res[k * Y * R : (k + 1) * Y * R]

        def second(s):
            lhs = half[pl.ds(s * 4, 4)].reshape(4 * Y * R, K * N)
            return jnp.dot(lhs, rcat[...], preferred_element_type=F32).reshape(4, Y, R, G * N)

        @pl.loop(0, S // 4)
        def _(s):
            if o == 0:
                d2d_out[h, pl.ds(s * 4, 4)] = second(s).astype(BF)
            else:
                own[h, pl.ds(s * 4, 4)] = second(s)

    def send_d2d(h):
        cp = term_copy(d2d_out.at[h], d2d_in.at[h], d2d_send.at[h], d2d_recv.at[h], sib)
        cp.start()
        pending.append(cp)
        return cp

    def send_y(h, d2d):
        d2d.wait_recv()
        copies = []
        for d in (2, 1, 3):
            to = lax.rem(y + d, Y)
            y_out[h, d - 1] = (own[h, :, to] + d2d_in[h, :, to].astype(F32)).astype(BF)
            cp = term_copy(
                y_out.at[h, d - 1], y_in.at[h, d - 1], y_send.at[h, d - 1], y_recv.at[h, d - 1], y_peer(d)
            )
            cp.start()
            copies.append(cp)
        pending.extend(copies)
        return copies

    def send_a2a(h, copies):
        for cp in copies:
            cp.wait_recv()
        total = own[h, :, y] + d2d_in[h, :, y].astype(F32)
        for d in range(1, Y):
            total = total + y_in[h, d - 1].astype(F32)
        total = total.astype(BF)
        for g in range(G):
            items[h, g * S : (g + 1) * S] = total[:, :, g * N : (g + 1) * N]

        @pl.loop(0, D)
        def _(p):
            a2a_out[h, p] = items[h, tab[p, 0]]

        a2a_in[h][me_s] = items[h, tab[me_s, 0]]

        @pl.loop(1, D)
        def _(q):
            p = lax.rem(me_s + q, D)
            pltpu.make_async_remote_copy(
                src_ref=a2a_out.at[h, p], dst_ref=a2a_in[h].at[me_s],
                send_sem=a2a_send.at[h], recv_sem=a2a_recv.at[h],
                device_id={"sector": p}, device_id_type=MESH,
            ).start()

    def combine(h):
        got = a2a_in[h].at[pl.ds(0, D - 1)]
        pltpu.make_async_copy(got, got, a2a_recv.at[h]).wait()
        first_row = me_t * (H * R) + h * R
        for t in range(S):
            value = a2a_in[h][tab[D + t, 0]].astype(F32) + a2a_in[h][tab[D + S + t, 0]].astype(F32)
            row_id = lax.broadcasted_iota(jnp.int32, (R, N), 0) + first_row
            value = jnp.where(row_id < rows[me_s * S + t], value, 0.0)
            out[t, h * R : (h + 1) * R] = value.astype(BF)

    unit(0, 0)
    d2d0 = send_d2d(0)
    unit(0, 1)
    y0 = send_y(0, d2d0)
    unit(1, 0)
    d2d1 = send_d2d(1)
    unit(1, 1)
    y1 = send_y(1, d2d1)
    tab_copy.wait()
    send_a2a(0, y0)
    send_a2a(1, y1)
    combine(0)
    combine(1)
    for cp in pending:
        cp.wait_send()
    for h in range(H):
        sent = a2a_out.at[h, pl.ds(0, D - 1)]
        pltpu.make_async_copy(sent, sent, a2a_send.at[h]).wait()


def local(wavefunction, left_ops, right_ops, term_type, target_slots, block_rows):
    left = left_ops.reshape(K, S, Y, 2, H, R, N)
    any_space = pl.BlockSpec(memory_space=pl.ANY)
    smem = pl.BlockSpec(memory_space=pltpu.SMEM)
    vmem = pl.BlockSpec(memory_space=pltpu.VMEM)
    dma = pltpu.SemaphoreType.DMA
    return pl.pallas_call(
        kernel,
        out_shape=jax.ShapeDtypeStruct((S, N // J, N), BF),
        in_specs=[any_space, any_space, any_space, smem, vmem, smem],
        out_specs=vmem,
        scratch_shapes=[
            pltpu.VMEM((H, 2, S, K, Y, R, N), BF),
            pltpu.VMEM((K, N, N), BF),
            pltpu.VMEM((K * N, G * N), BF),
            pltpu.VMEM((S, J, N // J, N), BF),
            pltpu.VMEM((S, N, N), BF),
            pltpu.VMEM((S, Y * R, K * N), BF),
            pltpu.VMEM((H, S, Y, R, G * N), F32),
            pltpu.VMEM((H, S, Y, R, G * N), BF),
            pltpu.VMEM((H, S, Y, R, G * N), BF),
            pltpu.VMEM((H, Y - 1, S, R, G * N), BF),
            pltpu.VMEM((H, Y - 1, S, R, G * N), BF),
            pltpu.VMEM((H, G * S, R, N), BF),
            pltpu.VMEM((H, D, R, N), BF),
            [pltpu.VMEM((D, R, N), BF)] * H,
            pltpu.VMEM((D + G * S, 128), jnp.int32),
            pltpu.SMEM((D + G * S, 128), jnp.int32),
            dma((H, 2, S)),
            dma((3,)),
            dma((C, 7)),
            dma((C, 7)),
            dma((H,)),
            dma((H,)),
            dma((H, Y - 1)),
            dma((H, Y - 1)),
            dma((H,)),
            dma((H,)),
        ],
        compiler_params=pltpu.CompilerParams(
            collective_id=0, has_side_effects=True, vmem_limit_bytes=56 * 1024 * 1024
        ),
    )(wavefunction, left, right_ops, term_type, target_slots, block_rows)


def solution(mesh):
    in_specs = (
        P("sector", "term", None),
        P("term", "sector", None, None),
        P("term", None, None),
        P("term"),
        P(),
        P(),
    )
    out_specs = P("sector", "term", None)
    return jax.shard_map(local, mesh=mesh, in_specs=in_specs, out_specs=out_specs, check_vma=False)
```

```python
import jax
import jax.numpy as jnp
from jax import lax
from jax.experimental import pallas as pl
from jax.experimental.pallas import tpu as pltpu
from jax.sharding import PartitionSpec as P

MESH = pl.DeviceIdType.MESH
BF, F32 = jnp.bfloat16, jnp.float32
N = 256
S = 8
K = 8
G = 2
Y = 4
J = 8
D = 32
H = 2
R = N // J // H
C = 4
SC = S // C
Q = 2
W = N // Q
X, Z = 4, 8
CHUNKS = [(h, q) for h in range(H) for q in range(Q)]
STEPS = sorted(
    ((dx, dz) for dx in range(X) for dz in range(Z) if dx or dz),
    key=lambda step: (-min(step[0], X - step[0]) - min(step[1], Z - step[1]), step[1] % 2, step),
)


def kernel(
    wf, left, right, types_h, slots_h, rows_h,
    out,
    left_v, right_v, rcat, gath, masked, half, own, d2d_out, d2d_in, y_out, y_in,
    items, a2a_out, a2a_in, tab_v, tab, types, slots, rows,
    left_sem, misc_sem, ag_send, ag_recv, d2d_send, d2d_recv, y_send, y_recv, a2a_send, a2a_recv, known,
):
    me_s, me_t = lax.axis_index("sector"), lax.axis_index("term")
    x, z, y, c = me_s // Z, me_s % Z, me_t // 2, me_t % 2
    sib = y * 2 + (1 - c)

    def y_peer(d):
        return lax.rem(y + d, Y) * 2 + c

    def z_peer(d):
        return x * Z + lax.rem(z + d, Z)

    def x_peer(d):
        return lax.rem(x + d, X) * Z + z

    def signal(sem, **to):
        pl.semaphore_signal(sem, inc=1, device_id=to, device_id_type=MESH)

    barrier = pltpu.get_barrier_semaphore()
    signal(barrier, term=sib)
    for d in range(1, Y):
        signal(barrier, term=y_peer(d))
    for d in (1, Z - 1):
        signal(barrier, sector=z_peer(d))
    for d in (1, X - 1):
        signal(barrier, sector=x_peer(d))

    def term_copy(src, dst, send, recv, to):
        return pltpu.make_async_remote_copy(
            src_ref=src, dst_ref=dst, send_sem=send, recv_sem=recv,
            device_id={"term": to}, device_id_type=MESH,
        )

    left_copies = {}

    def load(p):
        for h in range(H):
            for o in range(2):
                side = 1 - c if o == 0 else c
                cp = pltpu.make_async_copy(
                    left.at[:, pl.ds(p * SC, SC), :, side, h], left_v.at[p, h, o], left_sem.at[p, h, o]
                )
                cp.start()
                left_copies[p, h, o] = cp

    own_copy = pltpu.make_async_copy(wf, gath.at[:, me_t], misc_sem.at[1])
    own_copy.start()
    small = []
    for n, (src, dst) in enumerate(((slots_h, slots), (types_h, types), (rows_h, rows))):
        cp = pltpu.make_async_copy(src, dst, misc_sem.at[3 + n])
        cp.start()
        small.append(cp)
    right_copy = pltpu.make_async_copy(right, right_v, misc_sem.at[0])
    right_copy.start()
    load(0)
    own_copy.wait()
    pl.semaphore_wait(barrier, 1 + (Y - 1) + 4)

    pending = []
    first = {}
    for p in range(C):
        mine = gath.at[pl.ds(p * SC, SC), me_t]
        for d in (2, 1, 3):
            cp = term_copy(
                mine, mine, ag_send.at[p, d], ag_recv.at[p, d], y_peer(d)
            )
            cp.start()
            first[p, d] = cp
        cp = term_copy(mine, mine, ag_send.at[p, 0], ag_recv.at[p, 0], sib)
        cp.start()
        first[p, 0] = cp
    for d in (1, Z - 1):
        signal(known.at[0], sector=z_peer(d))
    for d in (1, X - 1):
        signal(known.at[0], sector=x_peer(d))
    for p in range(1, C):
        load(p)

    for cp in small:
        cp.wait()

    lane = lax.broadcasted_iota(jnp.int32, (D, D * S), 1)
    peer = lax.broadcasted_iota(jnp.int32, (D, D * S), 0)
    mine = lax.shift_right_logical(lane, 3) == me_s
    item = jnp.zeros((D, D * S), jnp.int32)
    target = lax.broadcasted_iota(jnp.int32, (S, D * S), 0) + me_s * S
    lane_s = lax.broadcasted_iota(jnp.int32, (S, D * S), 1)
    for g in range(G):
        row = slots[g : g + 1, :]
        hit = mine & (lax.shift_right_logical(row, 3) == peer)
        item = jnp.maximum(item, jnp.where(hit, jnp.bitwise_and(lane, 7) + g * S, 0))
        src = jnp.where(row == target, lax.shift_right_logical(lane_s, 3), 0)
        tab_v[D + g * S : D + (g + 1) * S, :] = jnp.broadcast_to(
            jnp.max(src, axis=1, keepdims=True), (S, 128)
        )
    tab_v[0:D, :] = jnp.broadcast_to(jnp.max(item, axis=1, keepdims=True), (D, 128))
    tab_copy = pltpu.make_async_copy(tab_v, tab, misc_sem.at[2])
    tab_copy.start()

    right_copy.wait()
    for k in range(K):
        for g in range(G):
            value = jnp.where(types[k] == g, right_v[k].astype(F32), 0.0).astype(BF)
            for q in range(Q):
                rcat[q, k * N : (k + 1) * N, g * W : (g + 1) * W] = value[:, q * W : (q + 1) * W]

    def forward(p):
        part = pl.ds(p * SC, SC)
        for d in (1, 3, 2):
            first[p, d].wait_recv()
            owner = lax.rem(y + Y - d, Y) * 2 + c
            block = gath.at[part, owner]
            cp = term_copy(block, block, ag_send.at[p, 3 + d], ag_recv.at[p, 3 + d], sib)
            cp.start()
            first[p, 3 + d] = cp

    def first_product(p):
        first[p, 0].wait_recv()
        for d in (1, 3, 2):
            first[p, 3 + d].wait_recv()
        for h in range(H):
            for o in range(2):
                left_copies[p, h, o].wait()
        row_id = lax.broadcasted_iota(jnp.int32, (N, N), 0)
        for s in range(p * SC, (p + 1) * SC):
            block = gath[s].reshape(N, N).astype(F32)
            masked[s] = jnp.where(row_id < rows[me_s * S + s], block, 0.0).astype(BF)
        for h in range(H):
            for o in range(2):
                for s in range(SC):
                    lhs = left_v[p, h, o, :, s].reshape(K * Y * R, N)
                    res = jnp.dot(lhs, masked[p * SC + s], preferred_element_type=F32).astype(BF)
                    for k in range(K):
                        half[h, o, p * SC + s, :, k * N : (k + 1) * N] = res[k * Y * R : (k + 1) * Y * R]

    def second_product(h, q, o, lo, n):
        lhs = half[h, o, lo : lo + n].reshape(n * Y * R, K * N)
        return jnp.dot(lhs, rcat[q], preferred_element_type=F32).reshape(n, Y, R, G * W)

    def products(i, p, lo, n):
        h, q = CHUNKS[i]
        d2d_out[i, lo : lo + n] = second_product(h, q, 0, lo, n).astype(BF)
        part = pl.ds(lo, n)
        cp = term_copy(d2d_out.at[i, part], d2d_in.at[i, part], d2d_send.at[i, p], d2d_recv.at[i, p], sib)
        cp.start()
        pending.append(cp)
        own[i, lo : lo + n] = second_product(h, q, 1, lo, n)
        return cp

    y_copies = {i: [] for i in range(len(CHUNKS))}

    def send_y(i, p, lo, n, d2d):
        d2d.wait_recv()
        part = pl.ds(lo, n)
        for d in (2, 1, 3):
            to = lax.rem(y + d, Y)
            y_out[i, d - 1, lo : lo + n] = (own[i, part, to] + d2d_in[i, part, to].astype(F32)).astype(BF)
            cp = term_copy(
                y_out.at[i, d - 1, part], y_in.at[i, d - 1, part],
                y_send.at[i, p, d - 1], y_recv.at[i, p, d - 1], y_peer(d),
            )
            cp.start()
            y_copies[i].append(cp)
            pending.append(cp)

    def send_a2a(i):
        for cp in y_copies[i]:
            cp.wait_recv()
        total = own[i, :, y] + d2d_in[i, :, y].astype(F32)
        for d in range(1, Y):
            total = total + y_in[i, d - 1].astype(F32)
        total = total.astype(BF)
        for g in range(G):
            items[i, g * S : (g + 1) * S] = total[:, :, g * W : (g + 1) * W]
        for dx, dz in STEPS:
            p = lax.rem(x + dx, X) * Z + lax.rem(z + dz, Z)
            a2a_out[i, p] = items[i, tab[p, 0]]
            pltpu.make_async_remote_copy(
                src_ref=a2a_out.at[i, p], dst_ref=a2a_in[i].at[me_s],
                send_sem=a2a_send.at[i], recv_sem=a2a_recv.at[i],
                device_id={"sector": p}, device_id_type=MESH,
            ).start()
        a2a_in[i][me_s] = items[i, tab[me_s, 0]]

    def combine(i):
        h, q = CHUNKS[i]
        got = a2a_in[i].at[pl.ds(0, D - 1)]
        pltpu.make_async_copy(got, got, a2a_recv.at[i]).wait()
        row_id = lax.broadcasted_iota(jnp.int32, (R, W), 0) + (me_t * (H * R) + h * R)
        for t in range(S):
            value = a2a_in[i][tab[D + t, 0]].astype(F32) + a2a_in[i][tab[D + S + t, 0]].astype(F32)
            value = jnp.where(row_id < rows[me_s * S + t], value, 0.0)
            out[t, h * R : (h + 1) * R, q * W : (q + 1) * W] = value.astype(BF)

    d2d = {}
    forward(0)
    for p in range(C):
        if p + 1 < C:
            forward(p + 1)
        first_product(p)
        d2d[p] = products(0, p, p * SC, SC)
        if p > 0:
            send_y(0, p - 1, (p - 1) * SC, SC, d2d[p - 1])
        if p == 0:
            pl.semaphore_wait(known.at[0], 4)
            for d in (2, Z - 2):
                signal(known.at[1], sector=z_peer(d))
        if p == 2:
            pl.semaphore_wait(known.at[1], 2)
            for d in range(1, X):
                signal(known.at[2], sector=x_peer(d))
    send_y(0, C - 1, (C - 1) * SC, SC, d2d[C - 1])
    pending += list(first.values())
    for i in range(1, len(CHUNKS)):
        send_y(i, 0, 0, S, products(i, 0, 0, S))
    tab_copy.wait()
    pl.semaphore_wait(known.at[2], X - 1)
    for i in range(len(CHUNKS)):
        send_a2a(i)
    for i in range(len(CHUNKS)):
        combine(i)
    for cp in pending:
        cp.wait_send()
    for i in range(H * Q):
        sent = a2a_out.at[i, pl.ds(0, D - 1)]
        pltpu.make_async_copy(sent, sent, a2a_send.at[i]).wait()


def local(wavefunction, left_ops, right_ops, term_type, target_slots, block_rows):
    left = left_ops.reshape(K, S, Y, 2, H, R, N)
    any_space = pl.BlockSpec(memory_space=pl.ANY)
    vmem = pl.BlockSpec(memory_space=pltpu.VMEM)
    dma = pltpu.SemaphoreType.DMA
    return pl.pallas_call(
        kernel,
        out_shape=pltpu.VMEM((S, N // J, N), BF),
        in_specs=[any_space] * 6,
        out_specs=vmem,
        scratch_shapes=[
            pltpu.VMEM((C, H, 2, K, SC, Y, R, N), BF),
            pltpu.VMEM((K, N, N), BF),
            pltpu.VMEM((Q, K * N, G * W), BF),
            pltpu.VMEM((S, J, N // J, N), BF),
            pltpu.VMEM((S, N, N), BF),
            pltpu.VMEM((H, 2, S, Y * R, K * N), BF),
            pltpu.VMEM((H * Q, S, Y, R, G * W), F32),
            pltpu.VMEM((H * Q, S, Y, R, G * W), BF),
            pltpu.VMEM((H * Q, S, Y, R, G * W), BF),
            pltpu.VMEM((H * Q, Y - 1, S, R, G * W), BF),
            pltpu.VMEM((H * Q, Y - 1, S, R, G * W), BF),
            pltpu.VMEM((H * Q, G * S, R, W), BF),
            pltpu.VMEM((H * Q, D, R, W), BF),
            [pltpu.VMEM((D, R, W), BF)] * (H * Q),
            pltpu.VMEM((D + G * S, 128), jnp.int32),
            pltpu.SMEM((D + G * S, 128), jnp.int32),
            pltpu.SMEM((K,), jnp.int32),
            pltpu.VMEM((G, D * S), jnp.int32),
            pltpu.SMEM((D * S,), jnp.int32),
            dma((C, H, 2)),
            dma((6,)),
            dma((C, 7)),
            dma((C, 7)),
            dma((H * Q, C)),
            dma((H * Q, C)),
            dma((H * Q, C, Y - 1)),
            dma((H * Q, C, Y - 1)),
            dma((H * Q,)),
            dma((H * Q,)),
            pltpu.SemaphoreType.REGULAR((3,)),
        ],
        compiler_params=pltpu.CompilerParams(
            collective_id=0, has_side_effects=True, vmem_limit_bytes=56 * 1024 * 1024
        ),
    )(wavefunction, left, right_ops, term_type, target_slots, block_rows)


def solution(mesh):
    in_specs = (
        P("sector", "term", None),
        P("term", "sector", None, None),
        P("term", None, None),
        P("term"),
        P(),
        P(),
    )
    out_specs = P("sector", "term", None)
    return jax.shard_map(local, mesh=mesh, in_specs=in_specs, out_specs=out_specs, check_vma=False)
```

```python
import jax
import jax.numpy as jnp
from jax import lax
from jax.experimental import pallas as pl
from jax.experimental.pallas import tpu as pltpu
from jax.sharding import PartitionSpec as P

MESH = pl.DeviceIdType.MESH
BF, F32 = jnp.bfloat16, jnp.float32
N = 256
S = 8
K = 8
G = 2
Y = 4
J = 8
D = 32
H = 2
R = N // J // H
C = 4
SC = S // C
Q = 2
W = N // Q
X, Z = 4, 8
CHUNKS = [(h, q) for q in range(Q) for h in range(H)]
STEPS = sorted(
    ((dx, dz) for dx in range(X) for dz in range(Z) if dx or dz),
    key=lambda step: (-min(step[0], X - step[0]) - min(step[1], Z - step[1]), step[1] % 2, step),
)


def kernel(
    wf, left, right, types_h, slots_h, rows_h,
    out,
    left_v, right_v, rcat, gath, masked, half, own, d2d_out, d2d_in, y_out, y_in,
    items, a2a_out, a2a_in, tab_v, tab, types, slots, rows,
    left_sem, misc_sem, ag_send, ag_recv, d2d_send, d2d_recv, y_send, y_recv, a2a_send, a2a_recv, known,
):
    me_s, me_t = lax.axis_index("sector"), lax.axis_index("term")
    x, z, y, c = me_s // Z, me_s % Z, me_t // 2, me_t % 2
    sib = y * 2 + (1 - c)

    def y_peer(d):
        return lax.rem(y + d, Y) * 2 + c

    def z_peer(d):
        return x * Z + lax.rem(z + d, Z)

    def x_peer(d):
        return lax.rem(x + d, X) * Z + z

    def signal(sem, **to):
        pl.semaphore_signal(sem, inc=1, device_id=to, device_id_type=MESH)

    barrier = pltpu.get_barrier_semaphore()
    signal(barrier, term=sib)
    for d in range(1, Y):
        signal(barrier, term=y_peer(d))
    for d in (1, Z - 1):
        signal(barrier, sector=z_peer(d))
    for d in (1, X - 1):
        signal(barrier, sector=x_peer(d))

    def term_copy(src, dst, send, recv, to):
        return pltpu.make_async_remote_copy(
            src_ref=src, dst_ref=dst, send_sem=send, recv_sem=recv,
            device_id={"term": to}, device_id_type=MESH,
        )

    left_copies = {}

    def load(p):
        for h in range(H):
            for o in range(2):
                side = 1 - c if o == 0 else c
                cp = pltpu.make_async_copy(
                    left.at[:, pl.ds(p * SC, SC), :, side, h], left_v.at[p, h, o], left_sem.at[p, h, o]
                )
                cp.start()
                left_copies[p, h, o] = cp

    own_copy = pltpu.make_async_copy(wf, gath.at[:, me_t], misc_sem.at[1])
    own_copy.start()
    small = []
    for n, (src, dst) in enumerate(((slots_h, slots), (types_h, types), (rows_h, rows))):
        cp = pltpu.make_async_copy(src, dst, misc_sem.at[3 + n])
        cp.start()
        small.append(cp)
    right_copy = pltpu.make_async_copy(right, right_v, misc_sem.at[0])
    right_copy.start()
    load(0)
    own_copy.wait()
    pl.semaphore_wait(barrier, 1 + (Y - 1) + 4)

    pending = []
    first = {}
    for p in range(C):
        mine = gath.at[pl.ds(p * SC, SC), me_t]
        for d in (2, 1, 3):
            cp = term_copy(
                mine, mine, ag_send.at[p, d], ag_recv.at[p, d], y_peer(d)
            )
            cp.start()
            first[p, d] = cp
        cp = term_copy(mine, mine, ag_send.at[p, 0], ag_recv.at[p, 0], sib)
        cp.start()
        first[p, 0] = cp
    for d in (1, Z - 1):
        signal(known.at[0], sector=z_peer(d))
    for d in (1, X - 1):
        signal(known.at[0], sector=x_peer(d))
    for p in range(1, C):
        load(p)

    for cp in small:
        cp.wait()

    lane = lax.broadcasted_iota(jnp.int32, (D, D * S), 1)
    peer = lax.broadcasted_iota(jnp.int32, (D, D * S), 0)
    mine = lax.shift_right_logical(lane, 3) == me_s
    item = jnp.zeros((D, D * S), jnp.int32)
    target = lax.broadcasted_iota(jnp.int32, (S, D * S), 0) + me_s * S
    lane_s = lax.broadcasted_iota(jnp.int32, (S, D * S), 1)
    for g in range(G):
        row = slots[g : g + 1, :]
        hit = mine & (lax.shift_right_logical(row, 3) == peer)
        item = jnp.maximum(item, jnp.where(hit, jnp.bitwise_and(lane, 7) + g * S, 0))
        src = jnp.where(row == target, lax.shift_right_logical(lane_s, 3), 0)
        tab_v[D + g * S : D + (g + 1) * S, :] = jnp.broadcast_to(
            jnp.max(src, axis=1, keepdims=True), (S, 128)
        )
    tab_v[0:D, :] = jnp.broadcast_to(jnp.max(item, axis=1, keepdims=True), (D, 128))
    tab_copy = pltpu.make_async_copy(tab_v, tab, misc_sem.at[2])
    tab_copy.start()

    right_copy.wait()
    for k in range(K):
        for g in range(G):
            value = jnp.where(types[k] == g, right_v[k].astype(F32), 0.0).astype(BF)
            for q in range(Q):
                rcat[q, k * N : (k + 1) * N, g * W : (g + 1) * W] = value[:, q * W : (q + 1) * W]

    def forward(p):
        part = pl.ds(p * SC, SC)
        for d in (1, 3, 2):
            first[p, d].wait_recv()
            owner = lax.rem(y + Y - d, Y) * 2 + c
            block = gath.at[part, owner]
            cp = term_copy(block, block, ag_send.at[p, 3 + d], ag_recv.at[p, 3 + d], sib)
            cp.start()
            first[p, 3 + d] = cp

    def first_product(p):
        first[p, 0].wait_recv()
        for d in (1, 3, 2):
            first[p, 3 + d].wait_recv()
        for h in range(H):
            for o in range(2):
                left_copies[p, h, o].wait()
        row_id = lax.broadcasted_iota(jnp.int32, (N, N), 0)
        for s in range(p * SC, (p + 1) * SC):
            block = gath[s].reshape(N, N).astype(F32)
            masked[s] = jnp.where(row_id < rows[me_s * S + s], block, 0.0).astype(BF)
        for h in range(H):
            for o in range(2):
                for s in range(SC):
                    lhs = left_v[p, h, o, :, s].reshape(K * Y * R, N)
                    res = jnp.dot(lhs, masked[p * SC + s], preferred_element_type=F32).astype(BF)
                    for k in range(K):
                        half[h, o, p * SC + s, :, k * N : (k + 1) * N] = res[k * Y * R : (k + 1) * Y * R]

    def second_product(q, lhs):
        shape = lhs.shape[:-2]
        res = jnp.dot(lhs.reshape(-1, K * N), rcat[q], preferred_element_type=F32)
        return res.reshape(shape + (Y, R, G * W))

    def send_d2d(q, p, lo, n):
        part = pl.ds(lo, n)
        cp = term_copy(
            d2d_out.at[q, :, part], d2d_in.at[q, :, part], d2d_send.at[q, p], d2d_recv.at[q, p], sib
        )
        cp.start()
        pending.append(cp)
        return cp

    y_copies = {chunk: [] for chunk in CHUNKS}

    def send_y(h, q, p, lo, n):
        part = pl.ds(lo, n)
        for d in (2, 1, 3):
            to = lax.rem(y + d, Y)
            value = own[q, h, part, to] + d2d_in[q, h, part, to].astype(F32)
            y_out[q, h, d - 1, lo : lo + n] = value.astype(BF)
            cp = term_copy(
                y_out.at[q, h, d - 1, part], y_in.at[q, h, d - 1, part],
                y_send.at[q, h, p, d - 1], y_recv.at[q, h, p, d - 1], y_peer(d),
            )
            cp.start()
            y_copies[h, q].append(cp)
            pending.append(cp)

    def send_a2a(i):
        h, q = CHUNKS[i]
        for cp in y_copies[h, q]:
            cp.wait_recv()
        total = own[q, h, :, y] + d2d_in[q, h, :, y].astype(F32)
        for d in range(1, Y):
            total = total + y_in[q, h, d - 1].astype(F32)
        total = total.astype(BF)
        for g in range(G):
            items[i, g * S : (g + 1) * S] = total[:, :, g * W : (g + 1) * W]
        for dx, dz in STEPS:
            p = lax.rem(x + dx, X) * Z + lax.rem(z + dz, Z)
            a2a_out[i, p] = items[i, tab[p, 0]]
            pltpu.make_async_remote_copy(
                src_ref=a2a_out.at[i, p], dst_ref=a2a_in[i].at[me_s],
                send_sem=a2a_send.at[i], recv_sem=a2a_recv.at[i],
                device_id={"sector": p}, device_id_type=MESH,
            ).start()
        a2a_in[i][me_s] = items[i, tab[me_s, 0]]

    def combine(i):
        h, q = CHUNKS[i]
        got = a2a_in[i].at[pl.ds(0, D - 1)]
        pltpu.make_async_copy(got, got, a2a_recv.at[i]).wait()
        row_id = lax.broadcasted_iota(jnp.int32, (R, W), 0) + (me_t * (H * R) + h * R)
        for t in range(S):
            value = a2a_in[i][tab[D + t, 0]].astype(F32) + a2a_in[i][tab[D + S + t, 0]].astype(F32)
            value = jnp.where(row_id < rows[me_s * S + t], value, 0.0)
            out[t, h * R : (h + 1) * R, q * W : (q + 1) * W] = value.astype(BF)

    shared = {}
    forward(0)
    for p in range(C):
        lo = p * SC
        if p + 1 < C:
            forward(p + 1)
        first_product(p)
        res = second_product(0, half[:, :, lo : lo + SC])
        d2d_out[0, :, lo : lo + SC] = res[:, 0].astype(BF)
        shared[p] = send_d2d(0, p, lo, SC)
        own[0, :, lo : lo + SC] = res[:, 1]
        if p > 0:
            shared[p - 1].wait_recv()
            send_y(0, 0, p - 1, lo - SC, SC)
        if p == 0:
            pl.semaphore_wait(known.at[0], 4)
            for d in (2, Z - 2):
                signal(known.at[1], sector=z_peer(d))
        if p == 2:
            pl.semaphore_wait(known.at[1], 2)
            for d in range(1, X):
                signal(known.at[2], sector=x_peer(d))
    pending += list(first.values())
    d2d_out[1, 0] = second_product(1, half[0, 0]).astype(BF)
    shared[C - 1].wait_recv()
    send_y(0, 0, C - 1, S - SC, SC)
    send_y(1, 0, 0, 0, S)
    d2d_out[1, 1] = second_product(1, half[1, 0]).astype(BF)
    right_half = send_d2d(1, 0, 0, S)
    own[1] = second_product(1, half[:, 1])
    right_half.wait_recv()
    for h in range(H):
        send_y(h, 1, 0, 0, S)
    tab_copy.wait()
    pl.semaphore_wait(known.at[2], X - 1)
    for i in range(len(CHUNKS)):
        send_a2a(i)
    for i in range(len(CHUNKS)):
        combine(i)
    for cp in pending:
        cp.wait_send()
    for i in range(H * Q):
        sent = a2a_out.at[i, pl.ds(0, D - 1)]
        pltpu.make_async_copy(sent, sent, a2a_send.at[i]).wait()


def local(wavefunction, left_ops, right_ops, term_type, target_slots, block_rows):
    left = left_ops.reshape(K, S, Y, 2, H, R, N)
    any_space = pl.BlockSpec(memory_space=pl.ANY)
    vmem = pl.BlockSpec(memory_space=pltpu.VMEM)
    dma = pltpu.SemaphoreType.DMA
    return pl.pallas_call(
        kernel,
        out_shape=pltpu.VMEM((S, N // J, N), BF),
        in_specs=[any_space] * 6,
        out_specs=vmem,
        scratch_shapes=[
            pltpu.VMEM((C, H, 2, K, SC, Y, R, N), BF),
            pltpu.VMEM((K, N, N), BF),
            pltpu.VMEM((Q, K * N, G * W), BF),
            pltpu.VMEM((S, J, N // J, N), BF),
            pltpu.VMEM((S, N, N), BF),
            pltpu.VMEM((H, 2, S, Y * R, K * N), BF),
            pltpu.VMEM((Q, H, S, Y, R, G * W), F32),
            pltpu.VMEM((Q, H, S, Y, R, G * W), BF),
            pltpu.VMEM((Q, H, S, Y, R, G * W), BF),
            pltpu.VMEM((Q, H, Y - 1, S, R, G * W), BF),
            pltpu.VMEM((Q, H, Y - 1, S, R, G * W), BF),
            pltpu.VMEM((H * Q, G * S, R, W), BF),
            pltpu.VMEM((H * Q, D, R, W), BF),
            [pltpu.VMEM((D, R, W), BF)] * (H * Q),
            pltpu.VMEM((D + G * S, 128), jnp.int32),
            pltpu.SMEM((D + G * S, 128), jnp.int32),
            pltpu.SMEM((K,), jnp.int32),
            pltpu.VMEM((G, D * S), jnp.int32),
            pltpu.SMEM((D * S,), jnp.int32),
            dma((C, H, 2)),
            dma((6,)),
            dma((C, 7)),
            dma((C, 7)),
            dma((Q, C)),
            dma((Q, C)),
            dma((Q, H, C, Y - 1)),
            dma((Q, H, C, Y - 1)),
            dma((H * Q,)),
            dma((H * Q,)),
            pltpu.SemaphoreType.REGULAR((3,)),
        ],
        compiler_params=pltpu.CompilerParams(
            collective_id=0, has_side_effects=True, vmem_limit_bytes=56 * 1024 * 1024
        ),
    )(wavefunction, left, right_ops, term_type, target_slots, block_rows)


def solution(mesh):
    in_specs = (
        P("sector", "term", None),
        P("term", "sector", None, None),
        P("term", None, None),
        P("term"),
        P(),
        P(),
    )
    out_specs = P("sector", "term", None)
    return jax.shard_map(local, mesh=mesh, in_specs=in_specs, out_specs=out_specs, check_vma=False)
```

```python
import jax
import jax.numpy as jnp
from jax import lax
from jax.experimental import pallas as pl
from jax.experimental.pallas import tpu as pltpu
from jax.sharding import PartitionSpec as P

MESH = pl.DeviceIdType.MESH
BF, F32 = jnp.bfloat16, jnp.float32
N = 256
S = 8
K = 8
G = 2
Y = 4
J = 8
D = 32
H = 2
R = N // J // H
PARTS = [(0, 2), (2, 2), (4, 2), (6, 1), (7, 1)]
C = len(PARTS)
Q = 2
W = N // Q
X, Z = 4, 8
CHUNKS = [(h, q) for q in range(Q) for h in range(H)]
STEPS = sorted(
    ((dx, dz) for dx in range(X) for dz in range(Z) if dx or dz),
    key=lambda step: (-min(step[0], X - step[0]) - min(step[1], Z - step[1]), step[1] % 2, step),
)


def kernel(
    wf, left, right, types_h, slots_h, rows_h,
    out,
    left_v, right_v, rcat, gath, masked, half, own, d2d_out, d2d_in, y_out, y_in,
    items, a2a_out, a2a_in, tab_v, tab, types, slots, rows,
    left_sem, misc_sem, ag_send, ag_recv, d2d_send, d2d_recv, y_send, y_recv, a2a_send, a2a_recv, known,
):
    me_s, me_t = lax.axis_index("sector"), lax.axis_index("term")
    x, z, y, c = me_s // Z, me_s % Z, me_t // 2, me_t % 2
    sib = y * 2 + (1 - c)

    def y_peer(d):
        return lax.rem(y + d, Y) * 2 + c

    def z_peer(d):
        return x * Z + lax.rem(z + d, Z)

    def x_peer(d):
        return lax.rem(x + d, X) * Z + z

    def signal(sem, **to):
        pl.semaphore_signal(sem, inc=1, device_id=to, device_id_type=MESH)

    barrier = pltpu.get_barrier_semaphore()
    signal(barrier, term=sib)
    for d in range(1, Y):
        signal(barrier, term=y_peer(d))
    for d in (1, Z - 1):
        signal(barrier, sector=z_peer(d))
    for d in (1, X - 1):
        signal(barrier, sector=x_peer(d))

    def term_copy(src, dst, send, recv, to):
        return pltpu.make_async_remote_copy(
            src_ref=src, dst_ref=dst, send_sem=send, recv_sem=recv,
            device_id={"term": to}, device_id_type=MESH,
        )

    left_copies = {}

    def load(p):
        slots_of = pl.ds(*PARTS[p])
        for h in range(H):
            for o in range(2):
                side = 1 - c if o == 0 else c
                cp = pltpu.make_async_copy(
                    left.at[:, slots_of, :, side, h], left_v.at[h, o, :, slots_of], left_sem.at[p, h, o]
                )
                cp.start()
                left_copies[p, h, o] = cp

    own_copy = pltpu.make_async_copy(wf, gath.at[:, me_t], misc_sem.at[1])
    own_copy.start()
    small = []
    for n, (src, dst) in enumerate(((slots_h, slots), (types_h, types), (rows_h, rows))):
        cp = pltpu.make_async_copy(src, dst, misc_sem.at[3 + n])
        cp.start()
        small.append(cp)
    right_copy = pltpu.make_async_copy(right, right_v, misc_sem.at[0])
    right_copy.start()
    load(0)
    own_copy.wait()
    pl.semaphore_wait(barrier, 1 + (Y - 1) + 4)

    pending = []
    first = {}
    for p in range(C):
        mine = gath.at[pl.ds(*PARTS[p]), me_t]
        for d in (2, 1, 3):
            cp = term_copy(
                mine, mine, ag_send.at[p, d], ag_recv.at[p, d], y_peer(d)
            )
            cp.start()
            first[p, d] = cp
        cp = term_copy(mine, mine, ag_send.at[p, 0], ag_recv.at[p, 0], sib)
        cp.start()
        first[p, 0] = cp
    for d in (1, Z - 1):
        signal(known.at[0], sector=z_peer(d))
    for d in (1, X - 1):
        signal(known.at[0], sector=x_peer(d))
    for p in range(1, C):
        load(p)

    for cp in small:
        cp.wait()

    lane = lax.broadcasted_iota(jnp.int32, (D, D * S), 1)
    peer = lax.broadcasted_iota(jnp.int32, (D, D * S), 0)
    mine = lax.shift_right_logical(lane, 3) == me_s
    item = jnp.zeros((D, D * S), jnp.int32)
    target = lax.broadcasted_iota(jnp.int32, (S, D * S), 0) + me_s * S
    lane_s = lax.broadcasted_iota(jnp.int32, (S, D * S), 1)
    for g in range(G):
        row = slots[g : g + 1, :]
        hit = mine & (lax.shift_right_logical(row, 3) == peer)
        item = jnp.maximum(item, jnp.where(hit, jnp.bitwise_and(lane, 7) + g * S, 0))
        src = jnp.where(row == target, lax.shift_right_logical(lane_s, 3), 0)
        tab_v[D + g * S : D + (g + 1) * S, :] = jnp.broadcast_to(
            jnp.max(src, axis=1, keepdims=True), (S, 128)
        )
    tab_v[0:D, :] = jnp.broadcast_to(jnp.max(item, axis=1, keepdims=True), (D, 128))
    tab_copy = pltpu.make_async_copy(tab_v, tab, misc_sem.at[2])
    tab_copy.start()

    right_copy.wait()
    for k in range(K):
        for g in range(G):
            value = jnp.where(types[k] == g, right_v[k].astype(F32), 0.0).astype(BF)
            for q in range(Q):
                rcat[q, k * N : (k + 1) * N, g * W : (g + 1) * W] = value[:, q * W : (q + 1) * W]

    def forward(p):
        part = pl.ds(*PARTS[p])
        for d in (1, 3, 2):
            first[p, d].wait_recv()
            owner = lax.rem(y + Y - d, Y) * 2 + c
            block = gath.at[part, owner]
            cp = term_copy(block, block, ag_send.at[p, 3 + d], ag_recv.at[p, 3 + d], sib)
            cp.start()
            first[p, 3 + d] = cp

    def first_product(p):
        first[p, 0].wait_recv()
        for d in (1, 3, 2):
            first[p, 3 + d].wait_recv()
        for h in range(H):
            for o in range(2):
                left_copies[p, h, o].wait()
        row_id = lax.broadcasted_iota(jnp.int32, (N, N), 0)
        lo, n = PARTS[p]
        for s in range(lo, lo + n):
            block = gath[s].reshape(N, N).astype(F32)
            masked[s] = jnp.where(row_id < rows[me_s * S + s], block, 0.0).astype(BF)
        for s in range(lo, lo + n):
            for h in range(H):
                for o in range(2):
                    lhs = left_v[h, o, :, s].reshape(K * Y * R, N)
                    res = jnp.dot(lhs, masked[s], preferred_element_type=F32).astype(BF)
                    for k in range(K):
                        half[h, o, s, :, k * N : (k + 1) * N] = res[k * Y * R : (k + 1) * Y * R]

    def second_product(q, lhs):
        shape = lhs.shape[:-2]
        res = jnp.dot(lhs.reshape(-1, K * N), rcat[q], preferred_element_type=F32)
        return res.reshape(shape + (Y, R, G * W))

    def send_d2d(q, h, nh, p, lo, n):
        at = (q, pl.ds(h, nh), pl.ds(lo, n))
        cp = term_copy(d2d_out.at[at], d2d_in.at[at], d2d_send.at[q, h, p], d2d_recv.at[q, h, p], sib)
        cp.start()
        pending.append(cp)
        return cp

    y_copies = {chunk: [] for chunk in CHUNKS}

    def send_y(h, q, p, lo, n):
        part = pl.ds(lo, n)
        for d in (2, 1, 3):
            to = lax.rem(y + d, Y)
            value = own[q, h, part, to] + d2d_in[q, h, part, to].astype(F32)
            y_out[q, h, d - 1, lo : lo + n] = value.astype(BF)
            cp = term_copy(
                y_out.at[q, h, d - 1, part], y_in.at[q, h, d - 1, part],
                y_send.at[q, h, p, d - 1], y_recv.at[q, h, p, d - 1], y_peer(d),
            )
            cp.start()
            y_copies[h, q].append(cp)
            pending.append(cp)

    def send_a2a(i):
        h, q = CHUNKS[i]
        for cp in y_copies[h, q]:
            cp.wait_recv()
        total = own[q, h, :, y] + d2d_in[q, h, :, y].astype(F32)
        for d in range(1, Y):
            total = total + y_in[q, h, d - 1].astype(F32)
        total = total.astype(BF)
        for g in range(G):
            items[i, g * S : (g + 1) * S] = total[:, :, g * W : (g + 1) * W]
        for at in range(0, len(STEPS), 8):
            peers = [
                lax.rem(x + dx, X) * Z + lax.rem(z + dz, Z) for dx, dz in STEPS[at : at + 8]
            ]
            picked = [items[i, tab[p, 0]] for p in peers]
            for p, value in zip(peers, picked):
                a2a_out[i, p] = value
            for p in peers:
                pltpu.make_async_remote_copy(
                    src_ref=a2a_out.at[i, p], dst_ref=a2a_in[i].at[me_s],
                    send_sem=a2a_send.at[i], recv_sem=a2a_recv.at[i],
                    device_id={"sector": p}, device_id_type=MESH,
                ).start()
        a2a_in[i][me_s] = items[i, tab[me_s, 0]]

    def combine(i):
        h, q = CHUNKS[i]
        got = a2a_in[i].at[pl.ds(0, D - 1)]
        pltpu.make_async_copy(got, got, a2a_recv.at[i]).wait()
        row_id = lax.broadcasted_iota(jnp.int32, (R, W), 0) + (me_t * (H * R) + h * R)
        both = [[a2a_in[i][tab[D + g * S + t, 0]] for g in range(G)] for t in range(S)]
        for t in range(S):
            value = both[t][0].astype(F32) + both[t][1].astype(F32)
            value = jnp.where(row_id < rows[me_s * S + t], value, 0.0)
            out[t, h * R : (h + 1) * R, q * W : (q + 1) * W] = value.astype(BF)

    shared = {}

    def send_y_part(p):
        shared[p].wait_recv()
        for h in range(H):
            send_y(h, 0, p, *PARTS[p])

    forward(0)
    for p in range(C):
        lo, n = PARTS[p]
        first_product(p)
        if p + 1 < C:
            forward(p + 1)
        res = second_product(0, half[:, :, lo : lo + n])
        d2d_out[0, :, lo : lo + n] = res[:, 0].astype(BF)
        shared[p] = send_d2d(0, 0, H, p, lo, n)
        own[0, :, lo : lo + n] = res[:, 1]
        if p > 0:
            send_y_part(p - 1)
        if p == 0:
            pl.semaphore_wait(known.at[0], 4)
            for d in (2, Z - 2):
                signal(known.at[1], sector=z_peer(d))
        if p == 2:
            pl.semaphore_wait(known.at[1], 2)
            for d in range(1, X):
                signal(known.at[2], sector=x_peer(d))
    pending += list(first.values())
    right_half = {}
    for h in range(H):
        d2d_out[1, h] = second_product(1, half[h, 0]).astype(BF)
        right_half[h] = send_d2d(1, h, 1, 0, 0, S)
        if h == 0:
            send_y_part(C - 1)
        else:
            right_half[0].wait_recv()
            send_y(0, 1, 0, 0, S)
        own[1, h] = second_product(1, half[h, 1])
    right_half[1].wait_recv()
    send_y(1, 1, 0, 0, S)
    tab_copy.wait()
    pl.semaphore_wait(known.at[2], X - 1)
    for i in range(len(CHUNKS)):
        send_a2a(i)
    for i in range(len(CHUNKS)):
        combine(i)
    for cp in pending:
        cp.wait_send()
    for i in range(H * Q):
        sent = a2a_out.at[i, pl.ds(0, D - 1)]
        pltpu.make_async_copy(sent, sent, a2a_send.at[i]).wait()


def local(wavefunction, left_ops, right_ops, term_type, target_slots, block_rows):
    left = left_ops.reshape(K, S, Y, 2, H, R, N)
    any_space = pl.BlockSpec(memory_space=pl.ANY)
    vmem = pl.BlockSpec(memory_space=pltpu.VMEM)
    dma = pltpu.SemaphoreType.DMA
    return pl.pallas_call(
        kernel,
        out_shape=pltpu.VMEM((S, N // J, N), BF),
        in_specs=[any_space] * 6,
        out_specs=vmem,
        scratch_shapes=[
            pltpu.VMEM((H, 2, K, S, Y, R, N), BF),
            pltpu.VMEM((K, N, N), BF),
            pltpu.VMEM((Q, K * N, G * W), BF),
            pltpu.VMEM((S, J, N // J, N), BF),
            pltpu.VMEM((S, N, N), BF),
            pltpu.VMEM((H, 2, S, Y * R, K * N), BF),
            pltpu.VMEM((Q, H, S, Y, R, G * W), F32),
            pltpu.VMEM((Q, H, S, Y, R, G * W), BF),
            pltpu.VMEM((Q, H, S, Y, R, G * W), BF),
            pltpu.VMEM((Q, H, Y - 1, S, R, G * W), BF),
            pltpu.VMEM((Q, H, Y - 1, S, R, G * W), BF),
            pltpu.VMEM((H * Q, G * S, R, W), BF),
            pltpu.VMEM((H * Q, D, R, W), BF),
            [pltpu.VMEM((D, R, W), BF)] * (H * Q),
            pltpu.VMEM((D + G * S, 128), jnp.int32),
            pltpu.SMEM((D + G * S, 128), jnp.int32),
            pltpu.SMEM((K,), jnp.int32),
            pltpu.VMEM((G, D * S), jnp.int32),
            pltpu.SMEM((D * S,), jnp.int32),
            dma((C, H, 2)),
            dma((6,)),
            dma((C, 7)),
            dma((C, 7)),
            dma((Q, H, C)),
            dma((Q, H, C)),
            dma((Q, H, C, Y - 1)),
            dma((Q, H, C, Y - 1)),
            dma((H * Q,)),
            dma((H * Q,)),
            pltpu.SemaphoreType.REGULAR((3,)),
        ],
        compiler_params=pltpu.CompilerParams(
            collective_id=0, has_side_effects=True, vmem_limit_bytes=56 * 1024 * 1024
        ),
    )(wavefunction, left, right_ops, term_type, target_slots, block_rows)


def solution(mesh):
    in_specs = (
        P("sector", "term", None),
        P("term", "sector", None, None),
        P("term", None, None),
        P("term"),
        P(),
        P(),
    )
    out_specs = P("sector", "term", None)
    return jax.shard_map(local, mesh=mesh, in_specs=in_specs, out_specs=out_specs, check_vma=False)
```

```python
import jax
import jax.numpy as jnp
from jax import lax
from jax.experimental import pallas as pl
from jax.experimental.pallas import tpu as pltpu
from jax.sharding import PartitionSpec as P

MESH = pl.DeviceIdType.MESH
BF, F32 = jnp.bfloat16, jnp.float32
N = 256
S = 8
K = 8
G = 2
Y = 4
J = 8
D = 32
H = 2
R = N // J // H
PARTS = [(0, 3), (3, 3), (6, 2)]
C = len(PARTS)
Q = 2
W = N // Q
X, Z = 4, 8
CHUNKS = [(h, q) for q in range(Q) for h in range(H)]
STEPS = sorted(
    ((dx, dz) for dx in range(X) for dz in range(Z) if dx or dz),
    key=lambda step: (-min(step[0], X - step[0]) - min(step[1], Z - step[1]), step[1] % 2, step),
)


def kernel(
    wf, left, right, types_h, slots_h, rows_h,
    out,
    left_v, right_v, rcat, gath, masked, half, own, d2d_out, d2d_in, y_out, y_in,
    items, a2a_out, a2a_in, tab_v, tab, types, slots, rows,
    left_sem, misc_sem, ag_send, ag_recv, d2d_send, d2d_recv, y_send, y_recv, a2a_send, a2a_recv, known,
):
    me_s, me_t = lax.axis_index("sector"), lax.axis_index("term")
    x, z, y, c = me_s // Z, me_s % Z, me_t // 2, me_t % 2
    sib = y * 2 + (1 - c)

    def y_peer(d):
        return lax.rem(y + d, Y) * 2 + c

    def z_peer(d):
        return x * Z + lax.rem(z + d, Z)

    def x_peer(d):
        return lax.rem(x + d, X) * Z + z

    def signal(sem, **to):
        pl.semaphore_signal(sem, inc=1, device_id=to, device_id_type=MESH)

    barrier = pltpu.get_barrier_semaphore()
    signal(barrier, term=sib)
    for d in range(1, Y):
        signal(barrier, term=y_peer(d))
    for d in (1, Z - 1):
        signal(barrier, sector=z_peer(d))
    for d in (1, X - 1):
        signal(barrier, sector=x_peer(d))

    def term_copy(src, dst, send, recv, to):
        return pltpu.make_async_remote_copy(
            src_ref=src, dst_ref=dst, send_sem=send, recv_sem=recv,
            device_id={"term": to}, device_id_type=MESH,
        )

    left_copies = {}

    def load(p):
        slots_of = pl.ds(*PARTS[p])
        for h in range(H):
            for o in range(2):
                side = 1 - c if o == 0 else c
                cp = pltpu.make_async_copy(
                    left.at[:, slots_of, :, side, h], left_v.at[h, o, :, slots_of], left_sem.at[p, h, o]
                )
                cp.start()
                left_copies[p, h, o] = cp

    own_copy = pltpu.make_async_copy(wf, gath.at[:, me_t], misc_sem.at[1])
    own_copy.start()
    small = []
    for n, (src, dst) in enumerate(((slots_h, slots), (types_h, types), (rows_h, rows))):
        cp = pltpu.make_async_copy(src, dst, misc_sem.at[3 + n])
        cp.start()
        small.append(cp)
    right_copy = pltpu.make_async_copy(right, right_v, misc_sem.at[0])
    right_copy.start()
    load(0)
    own_copy.wait()
    pl.semaphore_wait(barrier, 1 + (Y - 1) + 4)

    pending = []
    first = {}
    for p in range(C):
        mine = gath.at[pl.ds(*PARTS[p]), me_t]
        for d in (2, 1, 3):
            cp = term_copy(
                mine, mine, ag_send.at[p, d], ag_recv.at[p, d], y_peer(d)
            )
            cp.start()
            first[p, d] = cp
        cp = term_copy(mine, mine, ag_send.at[p, 0], ag_recv.at[p, 0], sib)
        cp.start()
        first[p, 0] = cp
    for d in (1, Z - 1):
        signal(known.at[0], sector=z_peer(d))
    for d in (1, X - 1):
        signal(known.at[0], sector=x_peer(d))
    for p in range(1, C):
        load(p)

    for cp in small:
        cp.wait()

    lane = lax.broadcasted_iota(jnp.int32, (D, D * S), 1)
    peer = lax.broadcasted_iota(jnp.int32, (D, D * S), 0)
    mine = lax.shift_right_logical(lane, 3) == me_s
    item = jnp.zeros((D, D * S), jnp.int32)
    target = lax.broadcasted_iota(jnp.int32, (S, D * S), 0) + me_s * S
    lane_s = lax.broadcasted_iota(jnp.int32, (S, D * S), 1)
    for g in range(G):
        row = slots[g : g + 1, :]
        hit = mine & (lax.shift_right_logical(row, 3) == peer)
        item = jnp.maximum(item, jnp.where(hit, jnp.bitwise_and(lane, 7) + g * S, 0))
        src = jnp.where(row == target, lax.shift_right_logical(lane_s, 3), 0)
        tab_v[D + g * S : D + (g + 1) * S, :] = jnp.broadcast_to(
            jnp.max(src, axis=1, keepdims=True), (S, 128)
        )
    tab_v[0:D, :] = jnp.broadcast_to(jnp.max(item, axis=1, keepdims=True), (D, 128))
    tab_copy = pltpu.make_async_copy(tab_v, tab, misc_sem.at[2])
    tab_copy.start()

    right_copy.wait()
    for k in range(K):
        for g in range(G):
            value = jnp.where(types[k] == g, right_v[k].astype(F32), 0.0).astype(BF)
            for q in range(Q):
                rcat[q, k * N : (k + 1) * N, g * W : (g + 1) * W] = value[:, q * W : (q + 1) * W]

    def forward(p):
        part = pl.ds(*PARTS[p])
        for d in (1, 3, 2):
            first[p, d].wait_recv()
            owner = lax.rem(y + Y - d, Y) * 2 + c
            block = gath.at[part, owner]
            cp = term_copy(block, block, ag_send.at[p, 3 + d], ag_recv.at[p, 3 + d], sib)
            cp.start()
            first[p, 3 + d] = cp

    def first_product(p):
        first[p, 0].wait_recv()
        for d in (1, 3, 2):
            first[p, 3 + d].wait_recv()
        for h in range(H):
            for o in range(2):
                left_copies[p, h, o].wait()
        row_id = lax.broadcasted_iota(jnp.int32, (N, N), 0)
        lo, n = PARTS[p]
        for s in range(lo, lo + n):
            block = gath[s].reshape(N, N).astype(F32)
            masked[s] = jnp.where(row_id < rows[me_s * S + s], block, 0.0).astype(BF)
        for s in range(lo, lo + n):
            for h in range(H):
                for o in range(2):
                    lhs = left_v[h, o, :, s].reshape(K * Y * R, N)
                    res = jnp.dot(lhs, masked[s], preferred_element_type=F32).astype(BF)
                    for k in range(K):
                        half[h, o, s, :, k * N : (k + 1) * N] = res[k * Y * R : (k + 1) * Y * R]

    def second_product(q, lhs):
        shape = lhs.shape[:-2]
        res = jnp.dot(lhs.reshape(-1, K * N), rcat[q], preferred_element_type=F32)
        return res.reshape(shape + (Y, R, G * W))

    def send_d2d(q, h, nh, p, lo, n):
        at = (q, pl.ds(h, nh), pl.ds(lo, n))
        cp = term_copy(d2d_out.at[at], d2d_in.at[at], d2d_send.at[q, h, p], d2d_recv.at[q, h, p], sib)
        cp.start()
        pending.append(cp)
        return cp

    y_copies = {chunk: [] for chunk in CHUNKS}

    def send_y(h, q, p, lo, n):
        part = pl.ds(lo, n)
        for d in (2, 1, 3):
            to = lax.rem(y + d, Y)
            value = own[q, h, part, to] + d2d_in[q, h, part, to].astype(F32)
            y_out[q, h, d - 1, lo : lo + n] = value.astype(BF)
            cp = term_copy(
                y_out.at[q, h, d - 1, part], y_in.at[q, h, d - 1, part],
                y_send.at[q, h, p, d - 1], y_recv.at[q, h, p, d - 1], y_peer(d),
            )
            cp.start()
            y_copies[h, q].append(cp)
            pending.append(cp)

    def send_a2a(i):
        h, q = CHUNKS[i]
        for cp in y_copies[h, q]:
            cp.wait_recv()
        total = own[q, h, :, y] + d2d_in[q, h, :, y].astype(F32)
        for d in range(1, Y):
            total = total + y_in[q, h, d - 1].astype(F32)
        total = total.astype(BF)
        for g in range(G):
            items[i, g * S : (g + 1) * S] = total[:, :, g * W : (g + 1) * W]
        for at in range(0, len(STEPS), 8):
            peers = [
                lax.rem(x + dx, X) * Z + lax.rem(z + dz, Z) for dx, dz in STEPS[at : at + 8]
            ]
            picked = [items[i, tab[p, 0]] for p in peers]
            for p, value in zip(peers, picked):
                a2a_out[i, p] = value
            for p in peers:
                pltpu.make_async_remote_copy(
                    src_ref=a2a_out.at[i, p], dst_ref=a2a_in[i].at[me_s],
                    send_sem=a2a_send.at[i], recv_sem=a2a_recv.at[i],
                    device_id={"sector": p}, device_id_type=MESH,
                ).start()
        a2a_in[i][me_s] = items[i, tab[me_s, 0]]

    def combine(i):
        h, q = CHUNKS[i]
        got = a2a_in[i].at[pl.ds(0, D - 1)]
        pltpu.make_async_copy(got, got, a2a_recv.at[i]).wait()
        row_id = lax.broadcasted_iota(jnp.int32, (R, W), 0) + (me_t * (H * R) + h * R)
        both = [[a2a_in[i][tab[D + g * S + t, 0]] for g in range(G)] for t in range(S)]
        for t in range(S):
            value = both[t][0].astype(F32) + both[t][1].astype(F32)
            value = jnp.where(row_id < rows[me_s * S + t], value, 0.0)
            out[t, h * R : (h + 1) * R, q * W : (q + 1) * W] = value.astype(BF)

    shared = {}

    def send_y_part(p):
        shared[p].wait_recv()
        for h in range(H):
            send_y(h, 0, p, *PARTS[p])

    forward(0)
    for p in range(C):
        lo, n = PARTS[p]
        first_product(p)
        if p + 1 < C:
            forward(p + 1)
        res = second_product(0, half[:, :, lo : lo + n])
        d2d_out[0, :, lo : lo + n] = res[:, 0].astype(BF)
        shared[p] = send_d2d(0, 0, H, p, lo, n)
        own[0, :, lo : lo + n] = res[:, 1]
        if p > 0:
            send_y_part(p - 1)
        if p == 0:
            pl.semaphore_wait(known.at[0], 4)
            for d in (2, Z - 2):
                signal(known.at[1], sector=z_peer(d))
        if p == 1:
            pl.semaphore_wait(known.at[1], 2)
            for d in range(1, X):
                signal(known.at[2], sector=x_peer(d))
    pending += list(first.values())
    right_half = {}
    for h in range(H):
        d2d_out[1, h] = second_product(1, half[h, 0]).astype(BF)
        right_half[h] = send_d2d(1, h, 1, 0, 0, S)
        if h == 0:
            send_y_part(C - 1)
        else:
            right_half[0].wait_recv()
            send_y(0, 1, 0, 0, S)
        own[1, h] = second_product(1, half[h, 1])
    right_half[1].wait_recv()
    send_y(1, 1, 0, 0, S)
    tab_copy.wait()
    pl.semaphore_wait(known.at[2], X - 1)
    for i in range(len(CHUNKS)):
        send_a2a(i)
    for i in range(len(CHUNKS)):
        combine(i)
    for cp in pending:
        cp.wait_send()
    for i in range(H * Q):
        sent = a2a_out.at[i, pl.ds(0, D - 1)]
        pltpu.make_async_copy(sent, sent, a2a_send.at[i]).wait()


def local(wavefunction, left_ops, right_ops, term_type, target_slots, block_rows):
    left = left_ops.reshape(K, S, Y, 2, H, R, N)
    any_space = pl.BlockSpec(memory_space=pl.ANY)
    vmem = pl.BlockSpec(memory_space=pltpu.VMEM)
    dma = pltpu.SemaphoreType.DMA
    return pl.pallas_call(
        kernel,
        out_shape=pltpu.VMEM((S, N // J, N), BF),
        in_specs=[any_space] * 6,
        out_specs=vmem,
        scratch_shapes=[
            pltpu.VMEM((H, 2, K, S, Y, R, N), BF),
            pltpu.VMEM((K, N, N), BF),
            pltpu.VMEM((Q, K * N, G * W), BF),
            pltpu.VMEM((S, J, N // J, N), BF),
            pltpu.VMEM((S, N, N), BF),
            pltpu.VMEM((H, 2, S, Y * R, K * N), BF),
            pltpu.VMEM((Q, H, S, Y, R, G * W), F32),
            pltpu.VMEM((Q, H, S, Y, R, G * W), BF),
            pltpu.VMEM((Q, H, S, Y, R, G * W), BF),
            pltpu.VMEM((Q, H, Y - 1, S, R, G * W), BF),
            pltpu.VMEM((Q, H, Y - 1, S, R, G * W), BF),
            pltpu.VMEM((H * Q, G * S, R, W), BF),
            pltpu.VMEM((H * Q, D, R, W), BF),
            [pltpu.VMEM((D, R, W), BF)] * (H * Q),
            pltpu.VMEM((D + G * S, 128), jnp.int32),
            pltpu.SMEM((D + G * S, 128), jnp.int32),
            pltpu.SMEM((K,), jnp.int32),
            pltpu.VMEM((G, D * S), jnp.int32),
            pltpu.SMEM((D * S,), jnp.int32),
            dma((C, H, 2)),
            dma((6,)),
            dma((C, 7)),
            dma((C, 7)),
            dma((Q, H, C)),
            dma((Q, H, C)),
            dma((Q, H, C, Y - 1)),
            dma((Q, H, C, Y - 1)),
            dma((H * Q,)),
            dma((H * Q,)),
            pltpu.SemaphoreType.REGULAR((3,)),
        ],
        compiler_params=pltpu.CompilerParams(
            collective_id=0, has_side_effects=True, vmem_limit_bytes=56 * 1024 * 1024
        ),
    )(wavefunction, left, right_ops, term_type, target_slots, block_rows)


def solution(mesh):
    in_specs = (
        P("sector", "term", None),
        P("term", "sector", None, None),
        P("term", None, None),
        P("term"),
        P(),
        P(),
    )
    out_specs = P("sector", "term", None)
    return jax.shard_map(local, mesh=mesh, in_specs=in_specs, out_specs=out_specs, check_vma=False)
```

```python
import jax
import jax.numpy as jnp
from jax import lax
from jax.experimental import pallas as pl
from jax.experimental.pallas import tpu as pltpu
from jax.sharding import PartitionSpec as P

MESH = pl.DeviceIdType.MESH
BF, F32 = jnp.bfloat16, jnp.float32
N = 256
S = 8
K = 8
G = 2
Y = 4
J = 8
D = 32
H = 2
R = N // J // H
PARTS = [(0, 3), (3, 3), (6, 2)]
C = len(PARTS)
Q = 2
W = N // Q
X, Z = 4, 8
CHUNKS = [(h, q) for q in range(Q) for h in range(H)]
STEPS = sorted(
    ((dx, dz) for dx in range(X) for dz in range(Z) if dx or dz),
    key=lambda step: (-min(step[0], X - step[0]) - min(step[1], Z - step[1]), step[1] % 2, step),
)


def kernel(
    wf, left, right, types_h, slots_h, rows_h,
    out,
    left_v, right_v, rcat, gath, masked, half, own, d2d_out, d2d_in, y_out, y_in,
    items, a2a_out, a2a_in, tab_v, tab, types, slots, rows,
    left_sem, misc_sem, ag_send, ag_recv, d2d_send, d2d_recv, y_send, y_recv, a2a_send, a2a_recv, known,
):
    me_s, me_t = lax.axis_index("sector"), lax.axis_index("term")
    x, z, y, c = me_s // Z, me_s % Z, me_t // 2, me_t % 2
    sib = y * 2 + (1 - c)

    def y_peer(d):
        return lax.rem(y + d, Y) * 2 + c

    def z_peer(d):
        return x * Z + lax.rem(z + d, Z)

    def x_peer(d):
        return lax.rem(x + d, X) * Z + z

    def signal(sem, **to):
        pl.semaphore_signal(sem, inc=1, device_id=to, device_id_type=MESH)

    barrier = pltpu.get_barrier_semaphore()
    signal(barrier, term=sib)
    for d in range(1, Y):
        signal(barrier, term=y_peer(d))
    for d in (1, Z - 1):
        signal(barrier, sector=z_peer(d))
    for d in (1, X - 1):
        signal(barrier, sector=x_peer(d))

    def term_copy(src, dst, send, recv, to):
        return pltpu.make_async_remote_copy(
            src_ref=src, dst_ref=dst, send_sem=send, recv_sem=recv,
            device_id={"term": to}, device_id_type=MESH,
        )

    left_copies = {}

    def load(p):
        slots_of = pl.ds(*PARTS[p])
        for h in range(H):
            for o in range(2):
                side = 1 - c if o == 0 else c
                cp = pltpu.make_async_copy(
                    left.at[:, slots_of, :, side, h], left_v.at[h, o, :, slots_of], left_sem.at[p, h, o]
                )
                cp.start()
                left_copies[p, h, o] = cp

    own_copy = pltpu.make_async_copy(wf, gath.at[:, me_t], misc_sem.at[1])
    own_copy.start()
    small = []
    for n, (src, dst) in enumerate(((slots_h, slots), (types_h, types), (rows_h, rows))):
        cp = pltpu.make_async_copy(src, dst, misc_sem.at[3 + n])
        cp.start()
        small.append(cp)
    right_copy = pltpu.make_async_copy(right, right_v, misc_sem.at[0])
    right_copy.start()
    load(0)
    own_copy.wait()
    pl.semaphore_wait(barrier, 1 + (Y - 1) + 4)

    pending = []
    first = {}
    for p in range(C):
        mine = gath.at[pl.ds(*PARTS[p]), me_t]
        for d in (2, 1, 3):
            cp = term_copy(
                mine, mine, ag_send.at[p, d], ag_recv.at[p, d], y_peer(d)
            )
            cp.start()
            first[p, d] = cp
        cp = term_copy(mine, mine, ag_send.at[p, 0], ag_recv.at[p, 0], sib)
        cp.start()
        first[p, 0] = cp
    for d in (1, Z - 1):
        signal(known.at[0], sector=z_peer(d))
    for d in (1, X - 1):
        signal(known.at[0], sector=x_peer(d))
    for p in range(1, C):
        load(p)

    for cp in small:
        cp.wait()

    lane = lax.broadcasted_iota(jnp.int32, (D, D * S), 1)
    peer = lax.broadcasted_iota(jnp.int32, (D, D * S), 0)
    mine = lax.shift_right_logical(lane, 3) == me_s
    item = jnp.zeros((D, D * S), jnp.int32)
    target = lax.broadcasted_iota(jnp.int32, (S, D * S), 0) + me_s * S
    lane_s = lax.broadcasted_iota(jnp.int32, (S, D * S), 1)
    for g in range(G):
        row = slots[g : g + 1, :]
        hit = mine & (lax.shift_right_logical(row, 3) == peer)
        item = jnp.maximum(item, jnp.where(hit, jnp.bitwise_and(lane, 7) + g * S, 0))
        src = jnp.where(row == target, lax.shift_right_logical(lane_s, 3), 0)
        tab_v[D + g * S : D + (g + 1) * S, :] = jnp.broadcast_to(
            jnp.max(src, axis=1, keepdims=True), (S, 128)
        )
    tab_v[0:D, :] = jnp.broadcast_to(jnp.max(item, axis=1, keepdims=True), (D, 128))
    tab_copy = pltpu.make_async_copy(tab_v, tab, misc_sem.at[2])
    tab_copy.start()

    right_copy.wait()
    for k in range(K):
        for g in range(G):
            value = jnp.where(types[k] == g, right_v[k].astype(F32), 0.0).astype(BF)
            for q in range(Q):
                rcat[q, k * N : (k + 1) * N, g * W : (g + 1) * W] = value[:, q * W : (q + 1) * W]

    def forward(p):
        part = pl.ds(*PARTS[p])
        for d in (1, 3, 2):
            first[p, d].wait_recv()
            owner = lax.rem(y + Y - d, Y) * 2 + c
            block = gath.at[part, owner]
            cp = term_copy(block, block, ag_send.at[p, 3 + d], ag_recv.at[p, 3 + d], sib)
            cp.start()
            first[p, 3 + d] = cp

    def first_product(p):
        first[p, 0].wait_recv()
        for d in (1, 3, 2):
            first[p, 3 + d].wait_recv()
        for h in range(H):
            for o in range(2):
                left_copies[p, h, o].wait()
        row_id = lax.broadcasted_iota(jnp.int32, (N, N), 0)
        lo, n = PARTS[p]
        for s in range(lo, lo + n):
            block = gath[s].reshape(N, N).astype(F32)
            masked[s] = jnp.where(row_id < rows[me_s * S + s], block, 0.0).astype(BF)
        for s in range(lo, lo + n):
            for h in range(H):
                for o in range(2):
                    lhs = left_v[h, o, :, s].reshape(K * Y * R, N)
                    res = jnp.dot(lhs, masked[s], preferred_element_type=F32).astype(BF)
                    for k in range(K):
                        half[h, o, s, :, k * N : (k + 1) * N] = res[k * Y * R : (k + 1) * Y * R]

    def second_product(q, lhs):
        shape = lhs.shape[:-2]
        res = jnp.dot(lhs.reshape(-1, K * N), rcat[q], preferred_element_type=F32)
        return res.reshape(shape + (Y, R, G * W))

    def send_d2d(q, h, nh, p, lo, n):
        at = (q, pl.ds(h, nh), pl.ds(lo, n))
        cp = term_copy(d2d_out.at[at], d2d_in.at[at], d2d_send.at[q, h, p], d2d_recv.at[q, h, p], sib)
        cp.start()
        pending.append(cp)
        return cp

    y_copies = {chunk: [] for chunk in CHUNKS}

    def send_y(h, q, p, lo, n):
        part = pl.ds(lo, n)
        for d in (2, 1, 3):
            to = lax.rem(y + d, Y)
            value = own[q, h, part, to] + d2d_in[q, h, part, to].astype(F32)
            y_out[q, h, d - 1, lo : lo + n] = value.astype(BF)
            cp = term_copy(
                y_out.at[q, h, d - 1, part], y_in.at[q, h, d - 1, part],
                y_send.at[q, h, p, d - 1], y_recv.at[q, h, p, d - 1], y_peer(d),
            )
            cp.start()
            y_copies[h, q].append(cp)
            pending.append(cp)

    def send_a2a(i):
        h, q = CHUNKS[i]
        for cp in y_copies[h, q]:
            cp.wait_recv()
        total = own[q, h, :, y] + d2d_in[q, h, :, y].astype(F32)
        for d in range(1, Y):
            total = total + y_in[q, h, d - 1].astype(F32)
        total = total.astype(BF)
        for g in range(G):
            items[i, g * S : (g + 1) * S] = total[:, :, g * W : (g + 1) * W]
        for at in range(0, len(STEPS), 8):
            peers = [
                lax.rem(x + dx, X) * Z + lax.rem(z + dz, Z) for dx, dz in STEPS[at : at + 8]
            ]
            picked = [items[i, tab[p, 0]] for p in peers]
            for p, value in zip(peers, picked):
                a2a_out[i, p] = value
            for p in peers:
                pltpu.make_async_remote_copy(
                    src_ref=a2a_out.at[i, p], dst_ref=a2a_in[i].at[me_s],
                    send_sem=a2a_send.at[i], recv_sem=a2a_recv.at[i],
                    device_id={"sector": p}, device_id_type=MESH,
                ).start()
        a2a_in[i][me_s] = items[i, tab[me_s, 0]]

    def combine(i):
        h, q = CHUNKS[i]
        got = a2a_in[i].at[pl.ds(0, D - 1)]
        pltpu.make_async_copy(got, got, a2a_recv.at[i]).wait()
        row_id = lax.broadcasted_iota(jnp.int32, (R, W), 0) + (me_t * (H * R) + h * R)
        both = [[a2a_in[i][tab[D + g * S + t, 0]] for g in range(G)] for t in range(S)]
        for t in range(S):
            value = both[t][0].astype(F32) + both[t][1].astype(F32)
            value = jnp.where(row_id < rows[me_s * S + t], value, 0.0)
            out[t, h * R : (h + 1) * R, q * W : (q + 1) * W] = value.astype(BF)

    shared = {}

    def send_y_part(p):
        shared[p].wait_recv()
        send_y(0, 0, p, *PARTS[p])

    forward(0)
    for p in range(C):
        lo, n = PARTS[p]
        first_product(p)
        if p + 1 < C:
            forward(p + 1)
        res = second_product(0, half[0, :, lo : lo + n])
        d2d_out[0, 0, lo : lo + n] = res[0].astype(BF)
        shared[p] = send_d2d(0, 0, 1, p, lo, n)
        own[0, 0, lo : lo + n] = res[1]
        if p > 0:
            send_y_part(p - 1)
        if p == 0:
            pl.semaphore_wait(known.at[0], 4)
            for d in (2, Z - 2):
                signal(known.at[1], sector=z_peer(d))
        if p == 1:
            pl.semaphore_wait(known.at[1], 2)
            for d in range(1, X):
                signal(known.at[2], sector=x_peer(d))
    pending += list(first.values())
    last = None
    for h, q in CHUNKS[1:]:
        d2d_out[q, h] = second_product(q, half[h, 0]).astype(BF)
        whole = send_d2d(q, h, 1, 0, 0, S)
        if last is None:
            send_y_part(C - 1)
        else:
            last[2].wait_recv()
            send_y(last[0], last[1], 0, 0, S)
        own[q, h] = second_product(q, half[h, 1])
        last = (h, q, whole)
    last[2].wait_recv()
    send_y(last[0], last[1], 0, 0, S)
    tab_copy.wait()
    pl.semaphore_wait(known.at[2], X - 1)
    for i in range(len(CHUNKS)):
        send_a2a(i)
    for i in range(len(CHUNKS)):
        combine(i)
    for cp in pending:
        cp.wait_send()
    for i in range(H * Q):
        sent = a2a_out.at[i, pl.ds(0, D - 1)]
        pltpu.make_async_copy(sent, sent, a2a_send.at[i]).wait()


def local(wavefunction, left_ops, right_ops, term_type, target_slots, block_rows):
    left = left_ops.reshape(K, S, Y, 2, H, R, N)
    any_space = pl.BlockSpec(memory_space=pl.ANY)
    vmem = pl.BlockSpec(memory_space=pltpu.VMEM)
    dma = pltpu.SemaphoreType.DMA
    return pl.pallas_call(
        kernel,
        out_shape=pltpu.VMEM((S, N // J, N), BF),
        in_specs=[any_space] * 6,
        out_specs=vmem,
        scratch_shapes=[
            pltpu.VMEM((H, 2, K, S, Y, R, N), BF),
            pltpu.VMEM((K, N, N), BF),
            pltpu.VMEM((Q, K * N, G * W), BF),
            pltpu.VMEM((S, J, N // J, N), BF),
            pltpu.VMEM((S, N, N), BF),
            pltpu.VMEM((H, 2, S, Y * R, K * N), BF),
            pltpu.VMEM((Q, H, S, Y, R, G * W), F32),
            pltpu.VMEM((Q, H, S, Y, R, G * W), BF),
            pltpu.VMEM((Q, H, S, Y, R, G * W), BF),
            pltpu.VMEM((Q, H, Y - 1, S, R, G * W), BF),
            pltpu.VMEM((Q, H, Y - 1, S, R, G * W), BF),
            pltpu.VMEM((H * Q, G * S, R, W), BF),
            pltpu.VMEM((H * Q, D, R, W), BF),
            [pltpu.VMEM((D, R, W), BF)] * (H * Q),
            pltpu.VMEM((D + G * S, 128), jnp.int32),
            pltpu.SMEM((D + G * S, 128), jnp.int32),
            pltpu.SMEM((K,), jnp.int32),
            pltpu.VMEM((G, D * S), jnp.int32),
            pltpu.SMEM((D * S,), jnp.int32),
            dma((C, H, 2)),
            dma((6,)),
            dma((C, 7)),
            dma((C, 7)),
            dma((Q, H, C)),
            dma((Q, H, C)),
            dma((Q, H, C, Y - 1)),
            dma((Q, H, C, Y - 1)),
            dma((H * Q,)),
            dma((H * Q,)),
            pltpu.SemaphoreType.REGULAR((3,)),
        ],
        compiler_params=pltpu.CompilerParams(
            collective_id=0, has_side_effects=True, vmem_limit_bytes=56 * 1024 * 1024
        ),
    )(wavefunction, left, right_ops, term_type, target_slots, block_rows)


def solution(mesh):
    in_specs = (
        P("sector", "term", None),
        P("term", "sector", None, None),
        P("term", None, None),
        P("term"),
        P(),
        P(),
    )
    out_specs = P("sector", "term", None)
    return jax.shard_map(local, mesh=mesh, in_specs=in_specs, out_specs=out_specs, check_vma=False)
```
